32 devices in a mesh: row: 4 (over y, x), col: 8 (over z, core).
Axes of the slice: x: 2, y: 2, z: 4, core: 2. Of those that a mesh axis runs over, the one named last changes fastest.
Arguments:
- factor: bfloat16 [4, 12, 512, 8, 1, 512], P('row', None, None, 'col'), may hold values from -0.03125 to 0.03125, as said below
- diag_inverse: float32 [4, 2, 1024, 512], P('row'), may hold values from -0.088388348 to 1.5, as said below
- residuals: float32 [256, 12, 4, 512], P('row', None, None, 'col'), may hold values from -6 to 6
Outputs:
- solved: float32 [256, 2, 4, 512], P('col', None, 'row')
- trailing: float32 [256, 10, 4, 512], P('col', None, 'row')
The draws below stay inside these ranges and needn't reach their ends.
Inputs may be any that keep to these rules, and one draw needn't show every extreme that they name: factor is zero wherever its row block halved (rounded down) is not above its column block halved. `diag_inverse`: each pair's inverse, assembled from its two blocks' columns, is lower triangular with diagonal entries from 0.5 to 1.5.
All inputs are finite; a program needn't handle non-finite values.
Results may differ from the reference program's by a relative error of at most 0.0095.
Values may be sent and summed in bfloat16 or wider, within the bound.
A program may use at most 64 MiB of HBM per device.

```python
import math
import jax
import jax.numpy as jnp
from jax import lax

NB = 512
W = 256
RBLK = 12
PANELS = 1
DROW = 2
N_ROW = 4
N_COL = 8


def draw_factor(key, part):
    array_shape = (N_ROW, RBLK, NB, N_COL, PANELS, NB)
    row_block = (jnp.arange(RBLK, dtype=jnp.int32)[None, :] * N_ROW + jnp.arange(N_ROW, dtype=jnp.int32)[:, None]).reshape(N_ROW, RBLK, 1, 1, 1, 1)
    col_block = (jnp.arange(PANELS, dtype=jnp.int32)[None, :] * N_COL + jnp.arange(N_COL, dtype=jnp.int32)[:, None]).reshape(1, 1, 1, N_COL, PANELS, 1)
    scale_value = 0.5 / math.sqrt(PANELS * N_COL * NB)
    entries = jax.random.truncated_normal(key, -4.0, 4.0, array_shape, jnp.float32)
    return jnp.where(row_block // 2 > col_block // 2, entries * scale_value, 0.0).astype(jnp.bfloat16)


def draw_diag_inverse(key, part):
    array_shape = (N_ROW, DROW, 2 * NB, NB)
    first_key = jax.random.fold_in(key, 11)
    second_key = jax.random.fold_in(key, 23)
    row_place = lax.broadcasted_iota(jnp.int32, array_shape, 2)
    parity = lax.broadcasted_iota(jnp.int32, array_shape, 0) % 2
    col_place = lax.broadcasted_iota(jnp.int32, array_shape, 3) + parity * NB
    scale_value = 0.5 / math.sqrt(NB)
    below = jax.random.truncated_normal(first_key, -4.0, 4.0, array_shape, jnp.float32)
    diagonal = jax.random.uniform(second_key, array_shape, jnp.float32, 0.6, 1.4)
    return jnp.where(row_place > col_place, below * scale_value, jnp.where(row_place == col_place, diagonal, 0.0)).astype(jnp.float32)


def block_scale(stream_key, shape, cuts, smallest, largest):
    gain, own = 1.0, jax.random.fold_in(stream_key, 6)
    for dim, blocks in cuts:
        draws = jnp.exp(jax.random.uniform(jax.random.fold_in(own, dim), (blocks,), jnp.float32, smallest / len(cuts), largest / len(cuts)))
        gain = gain * jnp.repeat(draws, shape[dim] // blocks).reshape([-1 if axis == dim else 1 for axis in range(len(shape))])
    return gain


def noise(rng, shape, scale, bound, shards=(), kind=jnp.bfloat16):
    level = block_scale(rng, shape, shards, -0.22, 0.18) if shards else 1.0
    array = jax.random.normal(rng, shape, jnp.float32) * scale * level
    return jnp.minimum(jnp.maximum(array, -bound), bound).astype(kind)


def setup_inputs(seed: int = 0) -> dict:
    seeds = jax.random.split(jax.random.key(seed), 4)
    return {
        "factor": draw_factor(jax.random.fold_in(seeds[3], 71), 0),
        "diag_inverse": draw_diag_inverse(jax.random.fold_in(seeds[3], 71), 0),
        "residuals": noise(seeds[2], (W, RBLK, N_ROW, NB), 1.0, 6.0, ((0, 4), (3, 8)), jnp.float32),
    }


def partial_sums(factor_block, known_blocks):
    partial_terms = jnp.einsum("rqbc,qbwc->qwr", factor_block.astype(jnp.float32), known_blocks.astype(jnp.float32))
    rounded = lax.optimization_barrier(partial_terms.astype(jnp.bfloat16))
    return jnp.sum(rounded.astype(jnp.float32), axis=0)


def reference(factor, diag_inverse, residuals):
    row_count = factor.shape[0]
    blocks_here = factor.shape[1]
    block_width = factor.shape[2]
    col_count = factor.shape[3]
    panel_count = factor.shape[4]
    walker_total = residuals.shape[0]
    diag_blocks = diag_inverse.shape[1]
    zero_index = jnp.int32(0)
    known_start = jnp.zeros((col_count, panel_count, walker_total, block_width), jnp.bfloat16)
    solved_start = jnp.zeros((walker_total, diag_blocks, row_count, block_width), jnp.float32)

    def block_input(block_index, known_blocks):
        local_block = (block_index // row_count).astype(jnp.int32)
        owner_row = (block_index % row_count).astype(jnp.int32)
        factor_block = lax.dynamic_slice(factor, (owner_row, local_block, zero_index, zero_index, zero_index, zero_index), (1, 1, block_width, col_count, panel_count, block_width))[0, 0]
        rhs_block = lax.dynamic_slice(residuals, (zero_index, local_block, owner_row, zero_index), (walker_total, 1, 1, block_width))[:, 0, 0, :]
        inverse = lax.dynamic_slice(diag_inverse, (owner_row, local_block, zero_index, zero_index), (1, 1, 2 * block_width, block_width))[0, 0]
        return jnp.dot(rhs_block - partial_sums(factor_block, known_blocks), inverse.T, precision=lax.Precision.HIGHEST, preferred_element_type=jnp.float32)

    def one_pair(pair_index, loop_state):
        known_blocks, solved_local = loop_state
        first_block = (2 * jnp.asarray(pair_index)).astype(jnp.int32)
        pair_solution = block_input(first_block, known_blocks) + block_input(first_block + 1, known_blocks)
        for half in range(2):
            block_index = (first_block + half).astype(jnp.int32)
            solution = pair_solution[:, half * block_width:(half + 1) * block_width]
            solved_local = lax.dynamic_update_slice(solved_local, solution[:, None, None, :], (zero_index, (block_index // row_count).astype(jnp.int32), (block_index % row_count).astype(jnp.int32), zero_index))
            known_blocks = lax.dynamic_update_slice(known_blocks, solution.astype(jnp.bfloat16)[None, None], ((block_index % col_count).astype(jnp.int32), (block_index // col_count).astype(jnp.int32), zero_index, zero_index))
        return known_blocks, solved_local

    known_blocks, solved_local = lax.fori_loop(0, panel_count * col_count // 2, one_pair, (known_start, solved_start))
    trailing_count = blocks_here - diag_blocks

    def trailing_block(flat_index):
        flat_index = flat_index.astype(jnp.int32)
        local_block = (diag_blocks + flat_index // row_count).astype(jnp.int32)
        owner_row = (flat_index % row_count).astype(jnp.int32)
        factor_block = lax.dynamic_slice(factor, (owner_row, local_block, zero_index, zero_index, zero_index, zero_index), (1, 1, block_width, col_count, panel_count, block_width))[0, 0]
        rhs_block = lax.dynamic_slice(residuals, (zero_index, local_block, owner_row, zero_index), (walker_total, 1, 1, block_width))[:, 0, 0, :]
        return rhs_block - partial_sums(factor_block, known_blocks)

    stacked = lax.map(trailing_block, jnp.arange(trailing_count * row_count, dtype=jnp.int32))
    trailing = stacked.reshape(trailing_count, row_count, walker_total, block_width).transpose(2, 0, 1, 3)
    return (solved_local, trailing)
```

```python
import functools

import jax
import jax.numpy as jnp
from jax import lax
from jax.experimental import pallas as pl
from jax.experimental.pallas import tpu as pltpu
from jax.sharding import PartitionSpec as P

MESH = pl.DeviceIdType.MESH
NT = (((1,), (1,)), ((), ()))


def dot_nt(x, w):
    return lax.dot_general(x, w, NT, preferred_element_type=jnp.float32)


def kernel(
    n_r,
    n_g,
    factor,
    inv,
    rhs,
    solved,
    trailing,
    lbuf,
    inv_hi,
    inv_lo,
    t_send,
    t_recv,
    y_send,
    ybuf,
    p_send,
    p_recv,
    s_l_own,
    s_l_send,
    s_l_recv,
    s_t_send,
    s_t_recv,
    s_y_send,
    s_y_recv,
    s_p_send,
    s_p_recv,
):
    p = lax.axis_index("row")
    q = lax.axis_index("col")
    g = q // 2
    c = q % 2
    n_a = rhs.shape[0]
    n_d = inv.shape[0]
    sw = rhs.shape[1]
    nb = rhs.shape[2]

    barrier = pltpu.get_barrier_semaphore()

    def greet(i, carry):
        pi, gi = i // n_g, i % n_g

        @pl.when(jnp.logical_or(pi != p, gi != g))
        def _():
            pl.semaphore_signal(
                barrier, inc=1, device_id=(pi, 2 * gi + c), device_id_type=MESH
            )

        return carry

    lax.fori_loop(0, n_r * n_g, greet, 0)
    pl.semaphore_signal(barrier, inc=1, device_id=(p, 2 * g + 1 - c), device_id_type=MESH)
    pl.semaphore_wait(barrier, n_r * n_g)

    def below(a):
        return (a * n_r + p) // 2 > g

    def l_own(a):
        return pltpu.make_async_copy(factor.at[a], lbuf.at[a, c], s_l_own.at[a])

    def l_other(a):
        return pltpu.make_async_remote_copy(
            src_ref=factor.at[a],
            dst_ref=lbuf.at[a, c],
            send_sem=s_l_send.at[a],
            recv_sem=s_l_recv.at[a],
            device_id=(p, 2 * g + 1 - c),
            device_id_type=MESH,
        )

    def l_arrived(a):
        return pltpu.make_async_remote_copy(
            src_ref=factor.at[a],
            dst_ref=lbuf.at[a, 1 - c],
            send_sem=s_l_send.at[a],
            recv_sem=s_l_recv.at[a],
            device_id=(p, 2 * g + 1 - c),
            device_id_type=MESH,
        )

    def l_start(a, carry):
        @pl.when(below(a))
        def _():
            l_own(a).start()
            l_other(a).start()

        return carry

    lax.fori_loop(0, n_a, l_start, 0)

    def split(d, carry):
        full = inv[d]
        hi = full.astype(jnp.bfloat16)
        inv_hi[d] = hi
        inv_lo[d] = (full - hi.astype(jnp.float32)).astype(jnp.bfloat16)
        return carry

    lax.fori_loop(0, n_d, split, 0)

    def part_copy(a, slot, to, at):
        return pltpu.make_async_remote_copy(
            src_ref=p_send.at[a, to],
            dst_ref=p_recv.at[a, slot],
            send_sem=s_p_send.at[a, to],
            recv_sem=s_p_recv.at[a, slot],
            device_id=(p, 2 * at + c),
            device_id_type=MESH,
        )

    def summed(a, count):
        def add(j, total):
            @pl.when(j != g)
            def _():
                part_copy(a, j, j, j).wait_recv()

            return total + p_recv[a, j].astype(jnp.float32)

        return lax.fori_loop(0, count, add, jnp.zeros((sw, nb), jnp.float32))

    def push(a, carry):
        @pl.when(below(a))
        def _():
            l_own(a).wait()
            l_arrived(a).wait_recv()
            x0 = ybuf[0].reshape(n_g * sw, nb)
            x1 = ybuf[1].reshape(n_g * sw, nb)
            part = dot_nt(x0, lbuf[a, 0]) + dot_nt(x1, lbuf[a, 1])
            p_send[a] = part.astype(jnp.bfloat16).reshape(n_g, sw, nb)
            for j in range(n_g):

                @pl.when(g != j)
                def _():
                    part_copy(a, g, j, j).start()

            p_recv[a, g] = p_send[a, g]

        return carry

    def t_copy(d, first):
        second = p - first
        return pltpu.make_async_remote_copy(
            src_ref=t_send.at[d],
            dst_ref=t_recv.at[d],
            send_sem=s_t_send.at[d],
            recv_sem=s_t_recv.at[d],
            device_id=(first + 1 - second, q),
            device_id_type=MESH,
        )

    def y_copy(d, second, m, to):
        return pltpu.make_async_remote_copy(
            src_ref=y_send.at[d],
            dst_ref=ybuf.at[second, g],
            send_sem=s_y_send.at[d, to],
            recv_sem=s_y_recv.at[second, g],
            device_id=(to, 2 * m + c),
            device_id_type=MESH,
        )

    def y_arrived(second, j):
        return pltpu.make_async_remote_copy(
            src_ref=y_send.at[0],
            dst_ref=ybuf.at[second, j],
            send_sem=s_y_send.at[0, 0],
            recv_sem=s_y_recv.at[second, j],
            device_id=(p, q),
            device_id_type=MESH,
        )

    def one_pair(m, carry):
        d = (2 * m) // n_r
        first = (2 * m) % n_r
        second = p - first
        owns = jnp.logical_or(p == first, p == first + 1)

        @pl.when(owns)
        def _():
            diff = rhs[d].astype(jnp.float32) - summed(d, m)
            hi = diff.astype(jnp.bfloat16)
            lo = (diff - hi.astype(jnp.float32)).astype(jnp.bfloat16)
            both = jnp.concatenate([hi, lo], axis=0)

            def half(start):
                rows = pl.ds(pl.multiple_of(start, nb), nb)
                wide = dot_nt(both, inv_hi[d, rows])
                return wide[:sw] + wide[sw:] + dot_nt(hi, inv_lo[d, rows])

            t_send[d] = half((1 - second) * nb)
            t_copy(d, first).start()
            mine = half(second * nb)
            t_copy(d, first).wait_recv()
            value = mine + t_recv[d]
            y_send[d] = value.astype(jnp.bfloat16)
            for to in range(n_r):

                @pl.when(jnp.logical_or(to != p, m != g))
                def _():
                    y_copy(d, second, m, to).start()

            solved[d] = value

            @pl.when(m == g)
            def _():
                ybuf[second, g] = y_send[d]

        @pl.when(m == g)
        def _():
            for j in range(n_g):
                for s in range(2):

                    @pl.when(jnp.logical_or(j != g, p != first + s))
                    def _():
                        y_arrived(s, j).wait_recv()

            lax.fori_loop(0, n_d, push, 0)

        @pl.when(m == g + 1)
        def _():
            lax.fori_loop(n_d, n_a, push, 0)

        return carry

    lax.fori_loop(0, n_g, one_pair, 0)

    @pl.when(g == n_g - 1)
    def _():
        lax.fori_loop(n_d, n_a, push, 0)

    def finish(a, carry):
        trailing[a - n_d] = rhs[a].astype(jnp.float32) - summed(a, n_g)
        return carry

    lax.fori_loop(n_d, n_a, finish, 0)

    def drain_pair(m, carry):
        d = (2 * m) // n_r
        first = (2 * m) % n_r
        second = p - first

        @pl.when(jnp.logical_or(p == first, p == first + 1))
        def _():
            t_copy(d, first).wait_send()
            for to in range(n_r):

                @pl.when(jnp.logical_or(to != p, m != g))
                def _():
                    y_copy(d, second, m, to).wait_send()

        return carry

    lax.fori_loop(0, n_g, drain_pair, 0)

    def drain_rows(a, carry):
        @pl.when(below(a))
        def _():
            l_other(a).wait_send()
            for j in range(n_g):

                @pl.when(g != j)
                def _():
                    part_copy(a, g, j, j).wait_send()

        return carry

    lax.fori_loop(0, n_a, drain_rows, 0)


def shards(factor, diag_inverse, residuals):
    n_r = lax.axis_size("row")
    n_col = lax.axis_size("col")
    n_g = n_col // 2
    flat = factor[0, :, :, 0, 0, :]
    n_a, nb = flat.shape[0], flat.shape[1]
    inverses = diag_inverse[0]
    n_d = inverses.shape[0]
    relaid = lax.all_to_all(
        lax.all_to_all(
            residuals.astype(jnp.bfloat16), "row", split_axis=2, concat_axis=0, tiled=True
        ),
        "col",
        split_axis=0,
        concat_axis=3,
        tiled=True,
    )
    rhs = relaid[:, :, 0, :].transpose(1, 0, 2)
    sw = rhs.shape[1]
    bf, f32 = jnp.bfloat16, jnp.float32
    vmem = pl.BlockSpec(memory_space=pltpu.VMEM)
    dma = pltpu.SemaphoreType.DMA
    solved, trailing = pl.pallas_call(
        functools.partial(kernel, n_r, n_g),
        out_shape=(
            jax.ShapeDtypeStruct((n_d, sw, nb), f32),
            jax.ShapeDtypeStruct((n_a - n_d, sw, nb), f32),
        ),
        in_specs=[pl.BlockSpec(memory_space=pl.ANY), vmem, vmem],
        out_specs=(vmem, vmem),
        scratch_shapes=[
            pltpu.VMEM((n_a, 2, nb, nb), bf),
            pltpu.VMEM(inverses.shape, bf),
            pltpu.VMEM(inverses.shape, bf),
            pltpu.VMEM((n_d, sw, nb), f32),
            pltpu.VMEM((n_d, sw, nb), f32),
            pltpu.VMEM((n_d, sw, nb), bf),
            pltpu.VMEM((2, n_g, sw, nb), bf),
            pltpu.VMEM((n_a, n_g, sw, nb), bf),
            pltpu.VMEM((n_a, n_g, sw, nb), bf),
            dma((n_a,)),
            dma((n_a,)),
            dma((n_a,)),
            dma((n_d,)),
            dma((n_d,)),
            dma((n_d, n_r)),
            dma((2, n_g)),
            dma((n_a, n_g)),
            dma((n_a, n_g)),
        ],
        compiler_params=pltpu.CompilerParams(
            collective_id=0, has_side_effects=True, vmem_limit_bytes=48 * 1024 * 1024
        ),
        cost_estimate=pl.CostEstimate(
            flops=2 * n_a * sw * n_g * 2 * nb * nb,
            bytes_accessed=2 * n_a * nb * nb * 2,
            transcendentals=0,
        ),
    )(flat, inverses, rhs)
    return (
        solved.transpose(1, 0, 2)[:, :, None, :],
        trailing.transpose(1, 0, 2)[:, :, None, :],
    )


def solution(mesh):
    placed = (
        P("row", None, None, "col", None, None),
        P("row", None, None, None),
        P("row", None, None, "col"),
    )
    return jax.shard_map(
        shards,
        mesh=mesh,
        in_specs=placed,
        out_specs=(P("col", None, "row", None), P("col", None, "row", None)),
        check_vma=False,
    )
```

```python
import functools

import jax
import jax.numpy as jnp
from jax import lax
from jax.experimental import pallas as pl
from jax.experimental.pallas import tpu as pltpu
from jax.sharding import PartitionSpec as P

MESH = pl.DeviceIdType.MESH
NT = (((1,), (1,)), ((), ()))


def dot_nt(x, w):
    return lax.dot_general(x, w, NT, preferred_element_type=jnp.float32)


def kernel(
    n_r,
    n_g,
    factor,
    inv_in,
    packed,
    solved,
    trailing,
    inv,
    rbuf,
    rhs,
    lbuf,
    inv_hi,
    inv_lo,
    t_send,
    t_recv,
    y_send,
    ybuf,
    p_send,
    p_recv,
    s_inv,
    s_r_own,
    s_r_send,
    s_r_recv,
    s_l_own,
    s_l_send,
    s_l_recv,
    s_t_send,
    s_t_recv,
    s_y_send,
    s_y_recv,
    s_p_send,
    s_p_recv,
):
    p = lax.axis_index("row")
    q = lax.axis_index("col")
    g = q // 2
    c = q % 2
    n_a = rhs.shape[0]
    n_d = inv.shape[0]
    sw = rhs.shape[1]
    nb = rhs.shape[2]

    n_col = 2 * n_g
    n_w = packed.shape[0]
    n_k = packed.shape[2]
    fold = n_a // n_k
    lw = nb // n_col
    n_u = -(-n_d // fold)

    def inv_copy(d):
        return pltpu.make_async_copy(inv_in.at[d], inv.at[d], s_inv.at[d])

    for d in range(n_d):
        inv_copy(d).start()

    barrier = pltpu.get_barrier_semaphore()

    def greet(i, carry):
        pi, qi = i // n_col, i % n_col

        @pl.when(jnp.logical_or(pi != p, qi != q))
        def _():
            pl.semaphore_signal(barrier, inc=1, device_id=(pi, qi), device_id_type=MESH)

        return carry

    lax.fori_loop(0, n_r * n_col, greet, 0)
    pl.semaphore_wait(barrier, n_r * n_col - 1)

    spans = (pl.ds(0, n_u), pl.ds(n_u, n_k - n_u))

    def r_copy(j, to, part):
        return pltpu.make_async_remote_copy(
            src_ref=packed.at[j, to, spans[part]],
            dst_ref=rbuf.at[q, spans[part]],
            send_sem=s_r_send.at[j, to, part],
            recv_sem=s_r_recv.at[q, part],
            device_id=(to, p * n_w + j),
            device_id_type=MESH,
        )

    def r_own(j, part):
        return pltpu.make_async_copy(
            packed.at[j, p, spans[part]], rbuf.at[q, spans[part]], s_r_own.at[part]
        )

    def r_arrived(j, part):
        return pltpu.make_async_remote_copy(
            src_ref=packed.at[0, 0, spans[part]],
            dst_ref=rbuf.at[j, spans[part]],
            send_sem=s_r_send.at[0, 0, part],
            recv_sem=s_r_recv.at[j, part],
            device_id=(p, q),
            device_id_type=MESH,
        )

    def r_start(part):
        for j in range(n_w):
            for to in range(n_r):
                here = jnp.logical_and(to == p, p * n_w + j == q)

                @pl.when(here)
                def _():
                    r_own(j, part).start()

                @pl.when(jnp.logical_not(here))
                def _():
                    r_copy(j, to, part).start()

    def r_wait(part):
        for j in range(n_col):
            here = jnp.logical_and(j == q, p == q // n_w)

            @pl.when(here)
            def _():
                r_own(q % n_w, part).wait()

            @pl.when(jnp.logical_not(here))
            def _():
                r_arrived(j, part).wait_recv()

    def unpack(k, carry):
        for j in range(n_col):
            piece = rbuf[j, k].astype(jnp.float32)
            for s in range(fold):
                rhs[k * fold + s, :, j * lw : (j + 1) * lw] = piece[:, s * lw : (s + 1) * lw]
        return carry

    def below(a):
        return (a * n_r + p) // 2 > g

    def l_own(a):
        return pltpu.make_async_copy(factor.at[a], lbuf.at[a, c], s_l_own.at[a])

    def l_other(a):
        return pltpu.make_async_remote_copy(
            src_ref=factor.at[a],
            dst_ref=lbuf.at[a, c],
            send_sem=s_l_send.at[a],
            recv_sem=s_l_recv.at[a],
            device_id=(p, 2 * g + 1 - c),
            device_id_type=MESH,
        )

    def l_arrived(a):
        return pltpu.make_async_remote_copy(
            src_ref=factor.at[a],
            dst_ref=lbuf.at[a, 1 - c],
            send_sem=s_l_send.at[a],
            recv_sem=s_l_recv.at[a],
            device_id=(p, 2 * g + 1 - c),
            device_id_type=MESH,
        )

    def l_start(a, carry):
        @pl.when(below(a))
        def _():
            l_own(a).start()
            l_other(a).start()

        return carry

    r_start(0)
    lax.fori_loop(0, n_d, l_start, 0)
    r_start(1)
    lax.fori_loop(n_d, n_a, l_start, 0)

    def split(d, carry):
        inv_copy(d).wait()
        full = inv[d]
        hi = full.astype(jnp.bfloat16)
        inv_hi[d] = hi
        inv_lo[d] = (full - hi.astype(jnp.float32)).astype(jnp.bfloat16)
        return carry

    split(0, 0)
    r_wait(0)
    lax.fori_loop(0, n_u, unpack, 0)

    def part_copy(a, slot, to, at):
        return pltpu.make_async_remote_copy(
            src_ref=p_send.at[a, to],
            dst_ref=p_recv.at[a, slot],
            send_sem=s_p_send.at[a, to],
            recv_sem=s_p_recv.at[a, slot],
            device_id=(p, 2 * at + c),
            device_id_type=MESH,
        )

    def summed(a, count):
        def add(j, total):
            @pl.when(j != g)
            def _():
                part_copy(a, j, j, j).wait_recv()

            return total + p_recv[a, j].astype(jnp.float32)

        return lax.fori_loop(0, count, add, jnp.zeros((sw, nb), jnp.float32))

    def push(a, carry):
        @pl.when(below(a))
        def _():
            l_own(a).wait()
            l_arrived(a).wait_recv()
            x0 = ybuf[0].reshape(n_g * sw, nb)
            x1 = ybuf[1].reshape(n_g * sw, nb)
            part = dot_nt(x0, lbuf[a, 0]) + dot_nt(x1, lbuf[a, 1])
            p_send[a] = part.astype(jnp.bfloat16).reshape(n_g, sw, nb)
            for j in range(n_g):

                @pl.when(g != j)
                def _():
                    part_copy(a, g, j, j).start()

            p_recv[a, g] = p_send[a, g]

        return carry

    def t_copy(d, first):
        second = p - first
        return pltpu.make_async_remote_copy(
            src_ref=t_send.at[d],
            dst_ref=t_recv.at[d],
            send_sem=s_t_send.at[d],
            recv_sem=s_t_recv.at[d],
            device_id=(first + 1 - second, q),
            device_id_type=MESH,
        )

    def y_copy(d, second, m, to):
        return pltpu.make_async_remote_copy(
            src_ref=y_send.at[d],
            dst_ref=ybuf.at[second, g],
            send_sem=s_y_send.at[d, to],
            recv_sem=s_y_recv.at[second, g],
            device_id=(to, 2 * m + c),
            device_id_type=MESH,
        )

    def y_arrived(second, j):
        return pltpu.make_async_remote_copy(
            src_ref=y_send.at[0],
            dst_ref=ybuf.at[second, j],
            send_sem=s_y_send.at[0, 0],
            recv_sem=s_y_recv.at[second, j],
            device_id=(p, q),
            device_id_type=MESH,
        )

    def one_pair(m, carry):
        d = (2 * m) // n_r
        first = (2 * m) % n_r
        second = p - first
        owns = jnp.logical_or(p == first, p == first + 1)

        @pl.when(owns)
        def _():
            diff = rhs[d] - summed(d, m)
            hi = diff.astype(jnp.bfloat16)
            lo = (diff - hi.astype(jnp.float32)).astype(jnp.bfloat16)
            both = jnp.concatenate([hi, lo], axis=0)

            def half(start):
                rows = pl.ds(pl.multiple_of(start, nb), nb)
                wide = dot_nt(both, inv_hi[d, rows])
                return wide[:sw] + wide[sw:] + dot_nt(hi, inv_lo[d, rows])

            t_send[d] = half((1 - second) * nb)
            t_copy(d, first).start()
            mine = half(second * nb)
            t_copy(d, first).wait_recv()
            value = mine + t_recv[d]
            y_send[d] = value.astype(jnp.bfloat16)
            for to in range(n_r):

                @pl.when(jnp.logical_or(to != p, m != g))
                def _():
                    y_copy(d, second, m, to).start()

            solved[d] = value

            @pl.when(m == g)
            def _():
                ybuf[second, g] = y_send[d]

        @pl.when(m == g)
        def _():
            for j in range(n_g):
                for s in range(2):

                    @pl.when(jnp.logical_or(j != g, p != first + s))
                    def _():
                        y_arrived(s, j).wait_recv()

            lax.fori_loop(0, n_d, push, 0)

        @pl.when(m == 0)
        def _():
            lax.fori_loop(1, n_d, split, 0)

        @pl.when(m == g + 1)
        def _():
            lax.fori_loop(n_d, n_a, push, 0)

        return carry

    lax.fori_loop(0, n_g, one_pair, 0)

    @pl.when(g == n_g - 1)
    def _():
        lax.fori_loop(n_d, n_a, push, 0)

    r_wait(1)
    lax.fori_loop(n_u, n_k, unpack, 0)

    def finish(a, carry):
        trailing[a - n_d] = rhs[a] - summed(a, n_g)
        return carry

    lax.fori_loop(n_d, n_a, finish, 0)

    for part in range(2):
        for j in range(n_w):
            for to in range(n_r):

                @pl.when(jnp.logical_or(to != p, p * n_w + j != q))
                def _():
                    r_copy(j, to, part).wait_send()

    def drain_pair(m, carry):
        d = (2 * m) // n_r
        first = (2 * m) % n_r
        second = p - first

        @pl.when(jnp.logical_or(p == first, p == first + 1))
        def _():
            t_copy(d, first).wait_send()
            for to in range(n_r):

                @pl.when(jnp.logical_or(to != p, m != g))
                def _():
                    y_copy(d, second, m, to).wait_send()

        return carry

    lax.fori_loop(0, n_g, drain_pair, 0)

    def drain_rows(a, carry):
        @pl.when(below(a))
        def _():
            l_other(a).wait_send()
            for j in range(n_g):

                @pl.when(g != j)
                def _():
                    part_copy(a, g, j, j).wait_send()

        return carry

    lax.fori_loop(0, n_a, drain_rows, 0)


def shards(factor, diag_inverse, residuals):
    n_r = lax.axis_size("row")
    n_col = lax.axis_size("col")
    n_g = n_col // 2
    flat = factor[0, :, :, 0, 0, :]
    n_a, nb = flat.shape[0], flat.shape[1]
    inverses = diag_inverse[0]
    n_d = inverses.shape[0]
    lw = nb // n_col
    fold = 128 // lw
    sw = residuals.shape[0] * n_r // n_col
    n_w = residuals.shape[0] // sw
    packed = (
        residuals.astype(jnp.bfloat16)
        .reshape(n_w, sw, n_a // fold, fold, n_r, lw)
        .transpose(0, 4, 2, 1, 3, 5)
        .reshape(n_w, n_r, n_a // fold, sw, fold * lw)
    )
    bf, f32 = jnp.bfloat16, jnp.float32
    vmem = pl.BlockSpec(memory_space=pltpu.VMEM)
    dma = pltpu.SemaphoreType.DMA
    solved, trailing = pl.pallas_call(
        functools.partial(kernel, n_r, n_g),
        out_shape=(
            jax.ShapeDtypeStruct((n_d, sw, nb), f32),
            jax.ShapeDtypeStruct((n_a - n_d, sw, nb), f32),
        ),
        in_specs=[pl.BlockSpec(memory_space=pl.ANY)] * 3,
        out_specs=(vmem, vmem),
        scratch_shapes=[
            pltpu.VMEM(inverses.shape, f32),
            pltpu.VMEM((n_col, n_a // fold, sw, fold * lw), bf),
            pltpu.VMEM((n_a, sw, nb), f32),
            pltpu.VMEM((n_a, 2, nb, nb), bf),
            pltpu.VMEM(inverses.shape, bf),
            pltpu.VMEM(inverses.shape, bf),
            pltpu.VMEM((n_d, sw, nb), f32),
            pltpu.VMEM((n_d, sw, nb), f32),
            pltpu.VMEM((n_d, sw, nb), bf),
            pltpu.VMEM((2, n_g, sw, nb), bf),
            pltpu.VMEM((n_a, n_g, sw, nb), bf),
            pltpu.VMEM((n_a, n_g, sw, nb), bf),
            dma((n_d,)),
            dma((2,)),
            dma((n_w, n_r, 2)),
            dma((n_col, 2)),
            dma((n_a,)),
            dma((n_a,)),
            dma((n_a,)),
            dma((n_d,)),
            dma((n_d,)),
            dma((n_d, n_r)),
            dma((2, n_g)),
            dma((n_a, n_g)),
            dma((n_a, n_g)),
        ],
        compiler_params=pltpu.CompilerParams(
            collective_id=0, has_side_effects=True, vmem_limit_bytes=60 * 1024 * 1024
        ),
        cost_estimate=pl.CostEstimate(
            flops=2 * n_a * sw * n_g * 2 * nb * nb,
            bytes_accessed=2 * n_a * nb * nb * 2,
            transcendentals=0,
        ),
    )(flat, inverses, packed)
    return (
        solved.transpose(1, 0, 2)[:, :, None, :],
        trailing.transpose(1, 0, 2)[:, :, None, :],
    )


def solution(mesh):
    placed = (
        P("row", None, None, "col", None, None),
        P("row", None, None, None),
        P("row", None, None, "col"),
    )
    return jax.shard_map(
        shards,
        mesh=mesh,
        in_specs=placed,
        out_specs=(P("col", None, "row", None), P("col", None, "row", None)),
        check_vma=False,
    )
```

```python
import functools

import jax
import jax.numpy as jnp
from jax import lax
from jax.experimental import pallas as pl
from jax.experimental.pallas import tpu as pltpu
from jax.sharding import PartitionSpec as P

MESH = pl.DeviceIdType.MESH
NT = (((1,), (1,)), ((), ()))


def dot_nt(x, w):
    return lax.dot_general(x, w, NT, preferred_element_type=jnp.float32)


def kernel(
    n_r,
    n_g,
    factor,
    inv_in,
    packed,
    solved,
    trailing,
    inv,
    mid,
    rbuf,
    rhs,
    lbuf,
    inv_hi,
    inv_lo,
    t_send,
    t_recv,
    y_send,
    ybuf,
    p_send,
    p_recv,
    s_inv,
    s_r_own,
    s_r_send,
    s_r_recv,
    s_m_own,
    s_m_send,
    s_m_recv,
    s_l_own,
    s_l_send,
    s_l_recv,
    s_t_send,
    s_t_recv,
    s_y_send,
    s_y_recv,
    s_p_send,
    s_p_recv,
):
    p = lax.axis_index("row")
    q = lax.axis_index("col")
    g = q // 2
    c = q % 2
    n_a = rhs.shape[0]
    n_d = inv.shape[0]
    sw = rhs.shape[1]
    nb = rhs.shape[2]

    n_col = 2 * n_g
    n_w = packed.shape[0]
    n_k = packed.shape[2]
    fold = n_a // n_k
    lw = nb // n_col
    n_u = -(-n_d // fold)

    def inv_copy(d):
        return pltpu.make_async_copy(inv_in.at[d], inv.at[d], s_inv.at[d])

    for d in range(n_d):
        inv_copy(d).start()

    barrier = pltpu.get_barrier_semaphore()

    def greet(i, carry):
        pi, qi = i // n_col, i % n_col

        @pl.when(jnp.logical_or(pi != p, qi != q))
        def _():
            pl.semaphore_signal(barrier, inc=1, device_id=(pi, qi), device_id_type=MESH)

        return carry

    lax.fori_loop(0, n_r * n_col, greet, 0)
    pl.semaphore_wait(barrier, n_r * n_col - 1)

    spans = (pl.ds(0, n_u), pl.ds(n_u, n_k - n_u))

    def r_here(j, to):
        return jnp.logical_and(to == p, p * n_w + j == q)

    def r_copy(j, to):
        return pltpu.make_async_remote_copy(
            src_ref=packed.at[j, to, spans[0]],
            dst_ref=rbuf.at[q, spans[0]],
            send_sem=s_r_send.at[j * n_r + to, 0],
            recv_sem=s_r_recv.at[q, 0],
            device_id=(to, p * n_w + j),
            device_id_type=MESH,
        )

    def r_own(part):
        src = packed.at[q % n_w, p, spans[0]] if part == 0 else mid.at[q // n_w, q % n_w]
        return pltpu.make_async_copy(src, rbuf.at[q, spans[part]], s_r_own.at[part])

    def r_arrived(j, part):
        return pltpu.make_async_remote_copy(
            src_ref=packed.at[0, 0, spans[part]],
            dst_ref=rbuf.at[j, spans[part]],
            send_sem=s_r_send.at[0, part],
            recv_sem=s_r_recv.at[j, part],
            device_id=(p, q),
            device_id_type=MESH,
        )

    def m_own():
        return pltpu.make_async_copy(packed.at[:, p, spans[1]], mid.at[p], s_m_own)

    def m_copy(to):
        return pltpu.make_async_remote_copy(
            src_ref=packed.at[:, to, spans[1]],
            dst_ref=mid.at[p],
            send_sem=s_m_send.at[to],
            recv_sem=s_m_recv.at[p],
            device_id=(to, q),
            device_id_type=MESH,
        )

    def m_arrived(j):
        return pltpu.make_async_remote_copy(
            src_ref=packed.at[:, 0, spans[1]],
            dst_ref=mid.at[j],
            send_sem=s_m_send.at[0],
            recv_sem=s_m_recv.at[j],
            device_id=(p, q),
            device_id_type=MESH,
        )

    def m_relay(to):
        return pltpu.make_async_remote_copy(
            src_ref=mid.at[to // n_w, to % n_w],
            dst_ref=rbuf.at[q, spans[1]],
            send_sem=s_r_send.at[to, 1],
            recv_sem=s_r_recv.at[q, 1],
            device_id=(p, to),
            device_id_type=MESH,
        )

    def r_start():
        for j in range(n_w):
            for to in range(n_r):

                @pl.when(jnp.logical_not(r_here(j, to)))
                def _():
                    r_copy(j, to).start()

        @pl.when(p == q // n_w)
        def _():
            r_own(0).start()

    def m_start():
        for to in range(n_r):

            @pl.when(to != p)
            def _():
                m_copy(to).start()

        m_own().start()

    def relay():
        m_own().wait()
        for j in range(n_r):

            @pl.when(j != p)
            def _():
                m_arrived(j).wait_recv()

        for j in range(n_col):

            @pl.when(j != q)
            def _():
                m_relay(j).start()

        r_own(1).start()

    def r_wait(part):
        for j in range(n_col):
            here = j == q
            if part == 0:
                here = jnp.logical_and(here, p == q // n_w)

            @pl.when(here)
            def _():
                r_own(part).wait()

            @pl.when(jnp.logical_not(here))
            def _():
                r_arrived(j, part).wait_recv()

    def unpack(k, carry):
        for j in range(n_col):
            piece = rbuf[j, k].astype(jnp.float32)
            for s in range(fold):
                rhs[k * fold + s, :, j * lw : (j + 1) * lw] = piece[:, s * lw : (s + 1) * lw]
        return carry

    def below(a):
        return (a * n_r + p) // 2 > g

    def l_own(a):
        return pltpu.make_async_copy(factor.at[a], lbuf.at[a, c], s_l_own.at[a])

    def l_other(a):
        return pltpu.make_async_remote_copy(
            src_ref=factor.at[a],
            dst_ref=lbuf.at[a, c],
            send_sem=s_l_send.at[a],
            recv_sem=s_l_recv.at[a],
            device_id=(p, 2 * g + 1 - c),
            device_id_type=MESH,
        )

    def l_arrived(a):
        return pltpu.make_async_remote_copy(
            src_ref=factor.at[a],
            dst_ref=lbuf.at[a, 1 - c],
            send_sem=s_l_send.at[a],
            recv_sem=s_l_recv.at[a],
            device_id=(p, 2 * g + 1 - c),
            device_id_type=MESH,
        )

    def l_start(a, carry):
        @pl.when(below(a))
        def _():
            l_own(a).start()
            l_other(a).start()

        return carry

    r_start()
    lax.fori_loop(0, n_d, l_start, 0)
    m_start()
    lax.fori_loop(n_d, n_a, l_start, 0)

    def split(d, carry):
        inv_copy(d).wait()
        full = inv[d]
        hi = full.astype(jnp.bfloat16)
        inv_hi[d] = hi
        inv_lo[d] = (full - hi.astype(jnp.float32)).astype(jnp.bfloat16)
        return carry

    split(0, 0)
    r_wait(0)
    lax.fori_loop(0, n_u, unpack, 0)

    def part_copy(a, slot, to, at):
        return pltpu.make_async_remote_copy(
            src_ref=p_send.at[a, to],
            dst_ref=p_recv.at[a, slot],
            send_sem=s_p_send.at[a, to],
            recv_sem=s_p_recv.at[a, slot],
            device_id=(p, 2 * at + c),
            device_id_type=MESH,
        )

    def summed(a, count):
        def add(j, total):
            @pl.when(j != g)
            def _():
                part_copy(a, j, j, j).wait_recv()

            return total + p_recv[a, j].astype(jnp.float32)

        return lax.fori_loop(0, count, add, jnp.zeros((sw, nb), jnp.float32))

    def push(a, carry):
        @pl.when(below(a))
        def _():
            l_own(a).wait()
            l_arrived(a).wait_recv()
            x0 = ybuf[0].reshape(n_g * sw, nb)
            x1 = ybuf[1].reshape(n_g * sw, nb)
            part = dot_nt(x0, lbuf[a, 0]) + dot_nt(x1, lbuf[a, 1])
            p_send[a] = part.astype(jnp.bfloat16).reshape(n_g, sw, nb)
            for j in range(n_g):

                @pl.when(g != j)
                def _():
                    part_copy(a, g, j, j).start()

            p_recv[a, g] = p_send[a, g]

        return carry

    def t_copy(d, first):
        second = p - first
        return pltpu.make_async_remote_copy(
            src_ref=t_send.at[d],
            dst_ref=t_recv.at[d],
            send_sem=s_t_send.at[d],
            recv_sem=s_t_recv.at[d],
            device_id=(first + 1 - second, q),
            device_id_type=MESH,
        )

    def y_copy(d, second, m, to):
        return pltpu.make_async_remote_copy(
            src_ref=y_send.at[d],
            dst_ref=ybuf.at[second, g],
            send_sem=s_y_send.at[d, to],
            recv_sem=s_y_recv.at[second, g],
            device_id=(to, 2 * m + c),
            device_id_type=MESH,
        )

    def y_arrived(second, j):
        return pltpu.make_async_remote_copy(
            src_ref=y_send.at[0],
            dst_ref=ybuf.at[second, j],
            send_sem=s_y_send.at[0, 0],
            recv_sem=s_y_recv.at[second, j],
            device_id=(p, q),
            device_id_type=MESH,
        )

    def one_pair(m, carry):
        d = (2 * m) // n_r
        first = (2 * m) % n_r
        second = p - first
        owns = jnp.logical_or(p == first, p == first + 1)

        @pl.when(owns)
        def _():
            diff = rhs[d] - summed(d, m)
            hi = diff.astype(jnp.bfloat16)
            lo = (diff - hi.astype(jnp.float32)).astype(jnp.bfloat16)
            both = jnp.concatenate([hi, lo], axis=0)

            def half(start):
                rows = pl.ds(pl.multiple_of(start, nb), nb)
                wide = dot_nt(both, inv_hi[d, rows])
                return wide[:sw] + wide[sw:] + dot_nt(hi, inv_lo[d, rows])

            t_send[d] = half((1 - second) * nb)
            t_copy(d, first).start()
            mine = half(second * nb)
            t_copy(d, first).wait_recv()
            value = mine + t_recv[d]
            y_send[d] = value.astype(jnp.bfloat16)
            for to in range(n_r):

                @pl.when(jnp.logical_or(to != p, m != g))
                def _():
                    y_copy(d, second, m, to).start()

            solved[d] = value

            @pl.when(m == g)
            def _():
                ybuf[second, g] = y_send[d]

        @pl.when(m == g)
        def _():
            for j in range(n_g):
                for s in range(2):

                    @pl.when(jnp.logical_or(j != g, p != first + s))
                    def _():
                        y_arrived(s, j).wait_recv()

            lax.fori_loop(0, n_d, push, 0)

        @pl.when(m == 0)
        def _():
            lax.fori_loop(1, n_d, split, 0)

        @pl.when(m == g + 1)
        def _():
            lax.fori_loop(n_d, n_a, push, 0)

        return carry

    relay()
    lax.fori_loop(0, n_g, one_pair, 0)

    @pl.when(g == n_g - 1)
    def _():
        lax.fori_loop(n_d, n_a, push, 0)

    r_wait(1)
    lax.fori_loop(n_u, n_k, unpack, 0)

    def finish(a, carry):
        trailing[a - n_d] = rhs[a] - summed(a, n_g)
        return carry

    lax.fori_loop(n_d, n_a, finish, 0)

    for j in range(n_w):
        for to in range(n_r):

            @pl.when(jnp.logical_not(r_here(j, to)))
            def _():
                r_copy(j, to).wait_send()

    for j in range(n_r):

        @pl.when(j != p)
        def _():
            m_copy(j).wait_send()

    for j in range(n_col):

        @pl.when(j != q)
        def _():
            m_relay(j).wait_send()

    def drain_pair(m, carry):
        d = (2 * m) // n_r
        first = (2 * m) % n_r
        second = p - first

        @pl.when(jnp.logical_or(p == first, p == first + 1))
        def _():
            t_copy(d, first).wait_send()
            for to in range(n_r):

                @pl.when(jnp.logical_or(to != p, m != g))
                def _():
                    y_copy(d, second, m, to).wait_send()

        return carry

    lax.fori_loop(0, n_g, drain_pair, 0)

    def drain_rows(a, carry):
        @pl.when(below(a))
        def _():
            l_other(a).wait_send()
            for j in range(n_g):

                @pl.when(g != j)
                def _():
                    part_copy(a, g, j, j).wait_send()

        return carry

    lax.fori_loop(0, n_a, drain_rows, 0)


def shards(factor, diag_inverse, residuals):
    n_r = lax.axis_size("row")
    n_col = lax.axis_size("col")
    n_g = n_col // 2
    flat = factor[0, :, :, 0, 0, :]
    n_a, nb = flat.shape[0], flat.shape[1]
    inverses = diag_inverse[0]
    n_d = inverses.shape[0]
    lw = nb // n_col
    fold = 128 // lw
    n_u = -(-n_d // fold)
    sw = residuals.shape[0] * n_r // n_col
    n_w = residuals.shape[0] // sw
    packed = (
        residuals.astype(jnp.bfloat16)
        .reshape(n_w, sw, n_a // fold, fold, n_r, lw)
        .transpose(0, 4, 2, 1, 3, 5)
        .reshape(n_w, n_r, n_a // fold, sw, fold * lw)
    )
    bf, f32 = jnp.bfloat16, jnp.float32
    vmem = pl.BlockSpec(memory_space=pltpu.VMEM)
    dma = pltpu.SemaphoreType.DMA
    solved, trailing = pl.pallas_call(
        functools.partial(kernel, n_r, n_g),
        out_shape=(
            jax.ShapeDtypeStruct((n_d, sw, nb), f32),
            jax.ShapeDtypeStruct((n_a - n_d, sw, nb), f32),
        ),
        in_specs=[pl.BlockSpec(memory_space=pl.ANY)] * 3,
        out_specs=(vmem, vmem),
        scratch_shapes=[
            pltpu.VMEM(inverses.shape, f32),
            pltpu.VMEM((n_r, n_w, n_a // fold - n_u, sw, fold * lw), bf),
            pltpu.VMEM((n_col, n_a // fold, sw, fold * lw), bf),
            pltpu.VMEM((n_a, sw, nb), f32),
            pltpu.VMEM((n_a, 2, nb, nb), bf),
            pltpu.VMEM(inverses.shape, bf),
            pltpu.VMEM(inverses.shape, bf),
            pltpu.VMEM((n_d, sw, nb), f32),
            pltpu.VMEM((n_d, sw, nb), f32),
            pltpu.VMEM((n_d, sw, nb), bf),
            pltpu.VMEM((2, n_g, sw, nb), bf),
            pltpu.VMEM((n_a, n_g, sw, nb), bf),
            pltpu.VMEM((n_a, n_g, sw, nb), bf),
            dma((n_d,)),
            dma((2,)),
            dma((n_col, 2)),
            dma((n_col, 2)),
            dma,
            dma((n_r,)),
            dma((n_r,)),
            dma((n_a,)),
            dma((n_a,)),
            dma((n_a,)),
            dma((n_d,)),
            dma((n_d,)),
            dma((n_d, n_r)),
            dma((2, n_g)),
            dma((n_a, n_g)),
            dma((n_a, n_g)),
        ],
        compiler_params=pltpu.CompilerParams(
            collective_id=0, has_side_effects=True, vmem_limit_bytes=60 * 1024 * 1024
        ),
        cost_estimate=pl.CostEstimate(
            flops=2 * n_a * sw * n_g * 2 * nb * nb,
            bytes_accessed=2 * n_a * nb * nb * 2,
            transcendentals=0,
        ),
    )(flat, inverses, packed)
    return (
        solved.transpose(1, 0, 2)[:, :, None, :],
        trailing.transpose(1, 0, 2)[:, :, None, :],
    )


def solution(mesh):
    placed = (
        P("row", None, None, "col", None, None),
        P("row", None, None, None),
        P("row", None, None, "col"),
    )
    return jax.shard_map(
        shards,
        mesh=mesh,
        in_specs=placed,
        out_specs=(P("col", None, "row", None), P("col", None, "row", None)),
        check_vma=False,
    )
```

```python
import functools

import jax
import jax.numpy as jnp
from jax import lax
from jax.experimental import pallas as pl
from jax.experimental.pallas import tpu as pltpu
from jax.sharding import PartitionSpec as P

MESH = pl.DeviceIdType.MESH
NT = (((1,), (1,)), ((), ()))


def dot_nt(x, w):
    return lax.dot_general(x, w, NT, preferred_element_type=jnp.float32)


def kernel(
    n_r,
    n_g,
    factor,
    inv_in,
    packed,
    solved,
    trailing,
    inv,
    mid,
    rbuf,
    rhs,
    lbuf,
    inv_hi,
    inv_lo,
    t_send,
    t_recv,
    y_send,
    ybuf,
    p_send,
    p_recv,
    s_inv,
    s_r_own,
    s_r_send,
    s_r_recv,
    s_m_own,
    s_m_send,
    s_m_recv,
    s_l_own,
    s_l_send,
    s_l_recv,
    s_t_send,
    s_t_recv,
    s_y_send,
    s_y_recv,
    s_y_pass,
    s_p_send,
    s_p_recv,
):
    p = lax.axis_index("row")
    q = lax.axis_index("col")
    g = q // 2
    c = q % 2
    n_a = rhs.shape[0]
    n_d = inv.shape[0]
    sw = rhs.shape[1]
    nb = rhs.shape[2]

    n_col = 2 * n_g
    n_w = packed.shape[0]
    n_k = packed.shape[2]
    fold = n_a // n_k
    lw = nb // n_col
    n_u = -(-n_d // fold)

    def inv_copy(d):
        return pltpu.make_async_copy(inv_in.at[d], inv.at[d], s_inv.at[d])

    for d in range(n_d):
        inv_copy(d).start()

    barrier = pltpu.get_barrier_semaphore()

    def greet(i, carry):
        pi, qi = i // n_col, i % n_col

        @pl.when(jnp.logical_or(pi != p, qi != q))
        def _():
            pl.semaphore_signal(barrier, inc=1, device_id=(pi, qi), device_id_type=MESH)

        return carry

    lax.fori_loop(0, n_r * n_col, greet, 0)
    pl.semaphore_wait(barrier, n_r * n_col - 1)

    spans = (pl.ds(0, n_u), pl.ds(n_u, n_k - n_u))

    def r_here(j, to):
        return jnp.logical_and(to == p, p * n_w + j == q)

    def r_copy(j, to):
        return pltpu.make_async_remote_copy(
            src_ref=packed.at[j, to, spans[0]],
            dst_ref=rbuf.at[q, spans[0]],
            send_sem=s_r_send.at[j * n_r + to, 0],
            recv_sem=s_r_recv.at[q, 0],
            device_id=(to, p * n_w + j),
            device_id_type=MESH,
        )

    def r_own(part):
        src = packed.at[q % n_w, p, spans[0]] if part == 0 else mid.at[q // n_w, q % n_w]
        return pltpu.make_async_copy(src, rbuf.at[q, spans[part]], s_r_own.at[part])

    def r_arrived(j, part):
        return pltpu.make_async_remote_copy(
            src_ref=packed.at[0, 0, spans[part]],
            dst_ref=rbuf.at[j, spans[part]],
            send_sem=s_r_send.at[0, part],
            recv_sem=s_r_recv.at[j, part],
            device_id=(p, q),
            device_id_type=MESH,
        )

    def m_own():
        return pltpu.make_async_copy(packed.at[:, p, spans[1]], mid.at[p], s_m_own)

    def m_copy(to):
        return pltpu.make_async_remote_copy(
            src_ref=packed.at[:, to, spans[1]],
            dst_ref=mid.at[p],
            send_sem=s_m_send.at[to],
            recv_sem=s_m_recv.at[p],
            device_id=(to, q),
            device_id_type=MESH,
        )

    def m_arrived(j):
        return pltpu.make_async_remote_copy(
            src_ref=packed.at[:, 0, spans[1]],
            dst_ref=mid.at[j],
            send_sem=s_m_send.at[0],
            recv_sem=s_m_recv.at[j],
            device_id=(p, q),
            device_id_type=MESH,
        )

    def m_relay(to):
        return pltpu.make_async_remote_copy(
            src_ref=mid.at[to // n_w, to % n_w],
            dst_ref=rbuf.at[q, spans[1]],
            send_sem=s_r_send.at[to, 1],
            recv_sem=s_r_recv.at[q, 1],
            device_id=(p, to),
            device_id_type=MESH,
        )

    def r_start():
        for j in range(n_w):
            for to in range(n_r):

                @pl.when(jnp.logical_not(r_here(j, to)))
                def _():
                    r_copy(j, to).start()

        @pl.when(p == q // n_w)
        def _():
            r_own(0).start()

    def m_start():
        for to in range(n_r):

            @pl.when(to != p)
            def _():
                m_copy(to).start()

        m_own().start()

    def relay():
        m_own().wait()
        for j in range(n_r):

            @pl.when(j != p)
            def _():
                m_arrived(j).wait_recv()

        for j in range(n_col):

            @pl.when(j != q)
            def _():
                m_relay(j).start()

        r_own(1).start()

    def r_wait(part):
        for j in range(n_col):
            here = j == q
            if part == 0:
                here = jnp.logical_and(here, p == q // n_w)

            @pl.when(here)
            def _():
                r_own(part).wait()

            @pl.when(jnp.logical_not(here))
            def _():
                r_arrived(j, part).wait_recv()

    def unpack(k, carry):
        for j in range(n_col):
            piece = rbuf[j, k].astype(jnp.float32)
            for s in range(fold):
                rhs[k * fold + s, :, j * lw : (j + 1) * lw] = piece[:, s * lw : (s + 1) * lw]
        return carry

    def below(a):
        return (a * n_r + p) // 2 > g

    def l_own(a):
        return pltpu.make_async_copy(factor.at[a], lbuf.at[a, c], s_l_own.at[a])

    def l_other(a):
        return pltpu.make_async_remote_copy(
            src_ref=factor.at[a],
            dst_ref=lbuf.at[a, c],
            send_sem=s_l_send.at[a],
            recv_sem=s_l_recv.at[a],
            device_id=(p, 2 * g + 1 - c),
            device_id_type=MESH,
        )

    def l_arrived(a):
        return pltpu.make_async_remote_copy(
            src_ref=factor.at[a],
            dst_ref=lbuf.at[a, 1 - c],
            send_sem=s_l_send.at[a],
            recv_sem=s_l_recv.at[a],
            device_id=(p, 2 * g + 1 - c),
            device_id_type=MESH,
        )

    def l_start(a, carry):
        @pl.when(below(a))
        def _():
            l_own(a).start()
            l_other(a).start()

        return carry

    r_start()
    lax.fori_loop(0, n_d, l_start, 0)
    m_start()
    lax.fori_loop(n_d, n_a, l_start, 0)

    def split(d, carry):
        inv_copy(d).wait()
        full = inv[d]
        hi = full.astype(jnp.bfloat16)
        inv_hi[d] = hi
        inv_lo[d] = (full - hi.astype(jnp.float32)).astype(jnp.bfloat16)
        return carry

    relay()
    split(0, 0)
    r_wait(0)
    lax.fori_loop(0, n_u, unpack, 0)

    def part_copy(a, slot, to, at):
        return pltpu.make_async_remote_copy(
            src_ref=p_send.at[a, to],
            dst_ref=p_recv.at[a, slot],
            send_sem=s_p_send.at[a, to],
            recv_sem=s_p_recv.at[a, slot],
            device_id=(p, 2 * at + c),
            device_id_type=MESH,
        )

    def summed(a, count):
        def add(j, total):
            @pl.when(j != g)
            def _():
                part_copy(a, j, j, j).wait_recv()

            return total + p_recv[a, j].astype(jnp.float32)

        return lax.fori_loop(0, count, add, jnp.zeros((sw, nb), jnp.float32))

    def push(a, carry):
        @pl.when(below(a))
        def _():
            l_own(a).wait()
            l_arrived(a).wait_recv()
            x0 = ybuf[0].reshape(n_g * sw, nb)
            x1 = ybuf[1].reshape(n_g * sw, nb)
            part = dot_nt(x0, lbuf[a, 0]) + dot_nt(x1, lbuf[a, 1])
            p_send[a] = part.astype(jnp.bfloat16).reshape(n_g, sw, nb)
            for j in range(n_g):

                @pl.when(g != j)
                def _():
                    part_copy(a, g, j, j).start()

            p_recv[a, g] = p_send[a, g]

        return carry

    def t_copy(d, first):
        second = p - first
        return pltpu.make_async_remote_copy(
            src_ref=t_send.at[d],
            dst_ref=t_recv.at[d],
            send_sem=s_t_send.at[d],
            recv_sem=s_t_recv.at[d],
            device_id=(first + 1 - second, q),
            device_id_type=MESH,
        )

    def y_copy(d, second, m, to):
        return pltpu.make_async_remote_copy(
            src_ref=y_send.at[d],
            dst_ref=ybuf.at[second, g],
            send_sem=s_y_send.at[d, to],
            recv_sem=s_y_recv.at[second, g],
            device_id=(to, 2 * m + c),
            device_id_type=MESH,
        )

    def y_pass(second, j, to):
        return pltpu.make_async_remote_copy(
            src_ref=ybuf.at[second, j],
            dst_ref=ybuf.at[second, j],
            send_sem=s_y_pass.at[j, to],
            recv_sem=s_y_recv.at[second, j],
            device_id=(to, q),
            device_id_type=MESH,
        )

    def y_arrived(second, j):
        return pltpu.make_async_remote_copy(
            src_ref=y_send.at[0],
            dst_ref=ybuf.at[second, j],
            send_sem=s_y_send.at[0, 0],
            recv_sem=s_y_recv.at[second, j],
            device_id=(p, q),
            device_id_type=MESH,
        )

    def one_pair(m, carry):
        d = (2 * m) // n_r
        first = (2 * m) % n_r
        second = p - first
        owns = jnp.logical_or(p == first, p == first + 1)

        @pl.when(owns)
        def _():
            diff = rhs[d] - summed(d, m)
            hi = diff.astype(jnp.bfloat16)
            lo = (diff - hi.astype(jnp.float32)).astype(jnp.bfloat16)
            both = jnp.concatenate([hi, lo], axis=0)

            def half(start):
                rows = pl.ds(pl.multiple_of(start, nb), nb)
                wide = dot_nt(both, inv_hi[d, rows])
                return wide[:sw] + wide[sw:] + dot_nt(hi, inv_lo[d, rows])

            t_send[d] = half((1 - second) * nb)
            t_copy(d, first).start()
            mine = half(second * nb)
            t_copy(d, first).wait_recv()
            value = mine + t_recv[d]
            y_send[d] = value.astype(jnp.bfloat16)

            @pl.when(m != g)
            def _():
                y_copy(d, second, m, p).start()

            solved[d] = value

            @pl.when(m == g)
            def _():
                ybuf[second, g] = y_send[d]

        @pl.when(m == g)
        def _():
            @pl.when(owns)
            def _():
                for i in range(n_g):
                    j = lax.rem(g + i, n_g)
                    if i:
                        y_arrived(second, j).wait_recv()
                    for to in range(n_r):

                        @pl.when(to != p)
                        def _():
                            y_pass(second, j, to).start()

            for j in range(n_g):
                for s in range(2):

                    @pl.when(p != first + s)
                    def _():
                        y_arrived(s, j).wait_recv()

            lax.fori_loop(0, n_d, push, 0)

        @pl.when(m == 0)
        def _():
            lax.fori_loop(1, n_d, split, 0)

        @pl.when(m > g)
        def _():
            left = n_a - n_d
            steps = jnp.maximum(n_g - 1 - g, 1)
            lax.fori_loop(
                n_d + left * (m - g - 1) // steps, n_d + left * (m - g) // steps, push, 0
            )

        return carry

    lax.fori_loop(0, n_g, one_pair, 0)

    @pl.when(g == n_g - 1)
    def _():
        lax.fori_loop(n_d, n_a, push, 0)

    r_wait(1)
    lax.fori_loop(n_u, n_k, unpack, 0)

    def finish(a, carry):
        trailing[a - n_d] = rhs[a] - summed(a, n_g)
        return carry

    lax.fori_loop(n_d, n_a, finish, 0)

    for j in range(n_w):
        for to in range(n_r):

            @pl.when(jnp.logical_not(r_here(j, to)))
            def _():
                r_copy(j, to).wait_send()

    for j in range(n_r):

        @pl.when(j != p)
        def _():
            m_copy(j).wait_send()

    for j in range(n_col):

        @pl.when(j != q)
        def _():
            m_relay(j).wait_send()

    def drain_pair(m, carry):
        d = (2 * m) // n_r
        first = (2 * m) % n_r
        second = p - first

        @pl.when(jnp.logical_or(p == first, p == first + 1))
        def _():
            t_copy(d, first).wait_send()

            @pl.when(m != g)
            def _():
                y_copy(d, second, m, p).wait_send()

            @pl.when(m == g)
            def _():
                for j in range(n_g):
                    for to in range(n_r):

                        @pl.when(to != p)
                        def _():
                            y_pass(second, j, to).wait_send()

        return carry

    lax.fori_loop(0, n_g, drain_pair, 0)

    def drain_rows(a, carry):
        @pl.when(below(a))
        def _():
            l_other(a).wait_send()
            for j in range(n_g):

                @pl.when(g != j)
                def _():
                    part_copy(a, g, j, j).wait_send()

        return carry

    lax.fori_loop(0, n_a, drain_rows, 0)


def shards(factor, diag_inverse, residuals):
    n_r = lax.axis_size("row")
    n_col = lax.axis_size("col")
    n_g = n_col // 2
    flat = factor[0, :, :, 0, 0, :]
    n_a, nb = flat.shape[0], flat.shape[1]
    inverses = diag_inverse[0]
    n_d = inverses.shape[0]
    lw = nb // n_col
    fold = 128 // lw
    n_u = -(-n_d // fold)
    sw = residuals.shape[0] * n_r // n_col
    n_w = residuals.shape[0] // sw
    packed = (
        residuals.astype(jnp.bfloat16)
        .reshape(n_w, sw, n_a // fold, fold, n_r, lw)
        .transpose(0, 4, 2, 1, 3, 5)
        .reshape(n_w, n_r, n_a // fold, sw, fold * lw)
    )
    bf, f32 = jnp.bfloat16, jnp.float32
    vmem = pl.BlockSpec(memory_space=pltpu.VMEM)
    dma = pltpu.SemaphoreType.DMA
    solved, trailing = pl.pallas_call(
        functools.partial(kernel, n_r, n_g),
        out_shape=(
            jax.ShapeDtypeStruct((n_d, sw, nb), f32),
            jax.ShapeDtypeStruct((n_a - n_d, sw, nb), f32),
        ),
        in_specs=[pl.BlockSpec(memory_space=pl.ANY)] * 3,
        out_specs=(vmem, vmem),
        scratch_shapes=[
            pltpu.VMEM(inverses.shape, f32),
            pltpu.VMEM((n_r, n_w, n_a // fold - n_u, sw, fold * lw), bf),
            pltpu.VMEM((n_col, n_a // fold, sw, fold * lw), bf),
            pltpu.VMEM((n_a, sw, nb), f32),
            pltpu.VMEM((n_a, 2, nb, nb), bf),
            pltpu.VMEM(inverses.shape, bf),
            pltpu.VMEM(inverses.shape, bf),
            pltpu.VMEM((n_d, sw, nb), f32),
            pltpu.VMEM((n_d, sw, nb), f32),
            pltpu.VMEM((n_d, sw, nb), bf),
            pltpu.VMEM((2, n_g, sw, nb), bf),
            pltpu.VMEM((n_a, n_g, sw, nb), bf),
            pltpu.VMEM((n_a, n_g, sw, nb), bf),
            dma((n_d,)),
            dma((2,)),
            dma((n_col, 2)),
            dma((n_col, 2)),
            dma,
            dma((n_r,)),
            dma((n_r,)),
            dma((n_a,)),
            dma((n_a,)),
            dma((n_a,)),
            dma((n_d,)),
            dma((n_d,)),
            dma((n_d, n_r)),
            dma((2, n_g)),
            dma((n_g, n_r)),
            dma((n_a, n_g)),
            dma((n_a, n_g)),
        ],
        compiler_params=pltpu.CompilerParams(
            collective_id=0, has_side_effects=True, vmem_limit_bytes=48 * 1024 * 1024
        ),
        cost_estimate=pl.CostEstimate(
            flops=2 * n_a * sw * n_g * 2 * nb * nb,
            bytes_accessed=2 * n_a * nb * nb * 2,
            transcendentals=0,
        ),
    )(flat, inverses, packed)
    return (
        solved.transpose(1, 0, 2)[:, :, None, :],
        trailing.transpose(1, 0, 2)[:, :, None, :],
    )


def solution(mesh):
    placed = (
        P("row", None, None, "col", None, None),
        P("row", None, None, None),
        P("row", None, None, "col"),
    )
    return jax.shard_map(
        shards,
        mesh=mesh,
        in_specs=placed,
        out_specs=(P("col", None, "row", None), P("col", None, "row", None)),
        check_vma=False,
    )
```
